32 devices in a mesh: dp: 8 (over z, x), tensor: 4 (over y, core).
Axes of the slice: x: 2, y: 2, z: 4, core: 2. Of those that a mesh axis runs over, the one named last changes fastest.
Arguments:
- tokens: bfloat16 [4096, 1024], P(('dp', 'tensor')), may hold values from -6 to 6
- segment_ids: int32 [8, 512], P('dp'), may hold values from 0 to 2, as said below
- positions: int32 [8, 512], P('dp'), may hold values from 0 to 511, as said below
- norm_in_gain: float32 [1024], replicated, may hold values from 0.5 to 1.5
- w_query: bfloat16 [1024, 1024], P('dp', 'tensor'), may hold values from -0.1875 to 0.1875
- w_key: bfloat16 [1024, 512], P('dp', 'tensor'), may hold values from -0.1875 to 0.1875
- w_value: bfloat16 [1024, 512], P('dp', 'tensor'), may hold values from -0.1875 to 0.1875
- query_gain: float32 [64], replicated, may hold values from 0.1 to 1.9
- key_gain: float32 [64], replicated, may hold values from 0.1 to 1.9
- w_output: bfloat16 [1024, 1024], P('tensor', 'dp'), may hold values from -0.75 to 0.75
- norm_mid_gain: float32 [1024], replicated, may hold values from 0.5 to 1.5
- w_gate: bfloat16 [1024, 4608], P('dp', 'tensor'), may hold values from -0.1875 to 0.1875
- w_up: bfloat16 [1024, 4608], P('dp', 'tensor'), may hold values from -0.1875 to 0.1875
- w_down: bfloat16 [4608, 1024], P('tensor', 'dp'), may hold values from -0.125 to 0.125
- grad_out: bfloat16 [4096, 1024], P(('dp', 'tensor')), may hold values from -6 to 6
Outputs:
- block_out: bfloat16 [4096, 1024], P(('dp', 'tensor'))
- grad_tokens: bfloat16 [4096, 1024], P(('dp', 'tensor'))
- grad_norm_in: float32 [1024], replicated
- grad_w_query: float32 [1024, 1024], P('dp', 'tensor')
- grad_w_key: float32 [1024, 512], P('dp', 'tensor')
- grad_w_value: float32 [1024, 512], P('dp', 'tensor')
- grad_query_gain: float32 [64], replicated
- grad_key_gain: float32 [64], replicated
- grad_w_output: float32 [1024, 1024], P('tensor', 'dp')
- grad_norm_mid: float32 [1024], replicated
- grad_w_gate: float32 [1024, 4608], P('dp', 'tensor')
- grad_w_up: float32 [1024, 4608], P('dp', 'tensor')
- grad_w_down: float32 [4608, 1024], P('tensor', 'dp')
The draws below stay inside these ranges and needn't reach their ends.
Inputs may be any that keep to these rules, and one draw needn't show every extreme that they name: `segment_ids`: within each sequence document numbers start at 0, never fall and rise by one at each new document; each sequence holds one to three documents, and one of them covers more than half of it; some sequence holds three. `positions`: each token's index within its document, counted from 0 at the document's first token; some sequence is a single document.
All inputs are finite; a program needn't handle non-finite values.
Results may differ from the reference program's by a relative error of at most 0.02.
Values may be sent and summed in bfloat16 or wider, within the bound.
No kernel may reach another device: no remote copies, remote signals or barrier semaphores. Data moves between devices by JAX's collectives and lax.ppermute only.
A program may use at most 128 MiB of HBM per device.

```python
import jax
import jax.numpy as jnp
from jax import lax

D = 1024
H = 16
KV = 8
HD = 64
FF = 4608
SEQ = 512
SEQS = 8
TOKENS = 4096


def layout(key):
    key_left, key_right = jax.random.split(key)
    quarter = SEQ // 4
    eighth = SEQ // 8
    left = jax.random.randint(key_left, (SEQS,), 0, quarter)
    right = jax.random.randint(key_right, (SEQS,), 0, quarter)
    left = jnp.where(left < eighth, 0, left)
    right = jnp.where(right < eighth, 0, right)
    rows = jnp.arange(SEQS)
    left = jnp.where(rows == 0, eighth + left % (quarter - eighth), left)
    right = jnp.where(rows == 0, eighth + right % (quarter - eighth), right)
    left = jnp.where(rows == SEQS - 1, 0, left)
    right = jnp.where(rows == SEQS - 1, 0, right)
    index = jnp.arange(SEQ)[None, :]
    start_big = left[:, None]
    end_big = SEQ - right[:, None]
    first = (left[:, None] > 0).astype(jnp.int32)
    segment = jnp.where(index < start_big, 0, jnp.where(index < end_big, first, first + 1))
    begin = jnp.where(index < start_big, 0, jnp.where(index < end_big, start_big, end_big))
    return (segment.astype(jnp.int32), (index - begin).astype(jnp.int32))


def draw_segment_ids(key, part):
    segment, place = layout(key)
    return segment


def draw_positions(key, part):
    segment, place = layout(key)
    return place


def with_spikes(array, own_key, source, target, parts, factor):
    owner, partner = [(jnp.arange(array.shape[dim]) // (array.shape[dim] // parts)).reshape([-1 if axis == dim else 1 for axis in range(array.ndim)]) for dim in (source, target)]
    chosen = jax.random.permutation(own_key, parts)[partner]
    strong = (owner == chosen) | (owner == (partner + parts // 2) % parts)
    return jnp.where(strong, factor * array, array)


def steps_of(rng, shape, cuts, low, top_value):
    level, own = 1.0, jax.random.fold_in(rng, 6)
    for position, blocks in cuts:
        steps = jnp.exp(jax.random.uniform(jax.random.fold_in(own, position), (blocks,), jnp.float32, low / len(cuts), top_value / len(cuts)))
        level = level * jnp.repeat(steps, shape[position] // blocks).reshape([-1 if axis == position else 1 for axis in range(len(shape))])
    return level


def gaussian(rng, shape, scale, most, cuts=(), kind=jnp.bfloat16):
    factor_of = steps_of(rng, shape, cuts, -0.22, 0.18) if cuts else 1.0
    values = jax.random.normal(rng, shape, jnp.float32) * scale * factor_of
    return jnp.minimum(jnp.maximum(values, -most), most).astype(kind)


def bell_draw_with(own_key, extent, deviation, most, shards, heavy, held_as=jnp.bfloat16):
    values = deviation * jax.random.normal(own_key, extent, jnp.float32)
    if shards:
        values = values * steps_of(own_key, extent, shards, -0.22, 0.18)
    return jnp.clip(with_spikes(values, jax.random.fold_in(own_key, 3), *heavy), -most, most).astype(held_as)


def setup_inputs(seed: int = 0) -> dict:
    keys = jax.random.split(jax.random.key(seed), 16)
    return {
        "tokens": gaussian(keys[0], (TOKENS, D), 1.0, 6.0, ((0, 32),)),
        "segment_ids": draw_segment_ids(jax.random.fold_in(keys[15], 71), 0),
        "positions": draw_positions(jax.random.fold_in(keys[15], 71), 0),
        "norm_in_gain": jnp.clip(1.0 + 0.1 * jax.random.normal(keys[3], (D,), jnp.float32), 0.5, 1.5),
        "w_query": gaussian(keys[4], (D, H * HD), D ** -0.5, 0.1875, ((0, 8), (1, 4))),
        "w_key": gaussian(keys[5], (D, KV * HD), D ** -0.5, 0.1875, ((0, 8), (1, 4))),
        "w_value": gaussian(keys[6], (D, KV * HD), D ** -0.5, 0.1875, ((0, 8), (1, 4))),
        "query_gain": jnp.clip(1.0 + 0.18 * jax.random.normal(keys[7], (HD,), jnp.float32), 0.1, 1.9),
        "key_gain": jnp.clip(1.0 + 0.18 * jax.random.normal(keys[8], (HD,), jnp.float32), 0.1, 1.9),
        "w_output": gaussian(keys[9], (H * HD, D), (H * HD // 16) ** -0.5, 0.75, ((0, 4), (1, 8))),
        "norm_mid_gain": jnp.clip(1.0 + 0.1 * jax.random.normal(keys[10], (D,), jnp.float32), 0.5, 1.5),
        "w_gate": gaussian(keys[11], (D, FF), D ** -0.5, 0.1875, ((0, 8), (1, 4))),
        "w_up": gaussian(keys[12], (D, FF), D ** -0.5, 0.1875, ((0, 8), (1, 4))),
        "w_down": gaussian(keys[13], (FF, D), (FF // 2) ** -0.5, 0.125, ((0, 4), (1, 8))),
        "grad_out": bell_draw_with(keys[14], (TOKENS, D), 1.0, 6.0, ((0, 32),), (0, 1, 32, 2.75)),
    }


@jax.custom_vjp
def low(v):
    return lax.optimization_barrier(v.astype(jnp.bfloat16)).astype(jnp.float32)

@jax.custom_vjp
def low_back(v):
    return v

def low_keep(v):
    return (low(v), None)

def low_pass(kept, grad):
    return (grad,)

def back_keep(v):
    return (v, None)

def back_low(kept, grad):
    return (low(grad),)
low.defvjp(low_keep, low_pass)
low_back.defvjp(back_keep, back_low)
EPSILON = 1e-05
HIGHEST = lax.Precision.HIGHEST

def matmul(left, right):
    return jnp.dot(left, right, precision=HIGHEST)

def normalize(values, gain):
    return values * lax.rsqrt(lax.optimization_barrier(jnp.mean(values * values, axis=-1, keepdims=True)) + EPSILON) * gain

def rotate(values, places):
    half = values.shape[-1] // 2
    steps = jnp.arange(half, dtype=jnp.float32) * (2.0 / values.shape[-1])
    freqs = jnp.power(jnp.float32(1000000.0), -steps)
    angles = places.astype(jnp.float32)[:, None] * freqs[None, :]
    cosine = jnp.cos(angles)[:, None, :]
    sine = jnp.sin(angles)[:, None, :]
    first = values[..., :half]
    second = values[..., half:]
    return jnp.concatenate([first * cosine - second * sine, second * cosine + first * sine], axis=-1)

def one_sequence(inputs, segment, places, norm_in_gain, w_query, w_key, w_value, query_gain, key_gain, w_output, norm_mid_gain, w_gate, w_up, w_down):
    count = inputs.shape[0]
    normed_in = low(normalize(inputs, norm_in_gain))
    query_raw = low_back(matmul(normed_in, w_query)).reshape(count, H, HD)
    key_raw = low_back(matmul(normed_in, w_key)).reshape(count, KV, HD)
    values = low(low_back(matmul(normed_in, w_value))).reshape(count, KV, HD)
    query = low(rotate(normalize(query_raw, query_gain), places))
    key = low(rotate(normalize(key_raw, key_gain), places))
    key_wide = jnp.repeat(key, H // KV, axis=1)
    value_wide = jnp.repeat(values, H // KV, axis=1)
    scores = low_back(jnp.einsum('qhd,khd->hqk', query, key_wide, precision=HIGHEST) * HD ** (-0.5))
    index = jnp.arange(count)
    allowed = (segment[:, None] == segment[None, :]) & (index[None, :] <= index[:, None])
    scores = jnp.where(allowed[None], scores, -1e+30)
    weights = jnp.exp(scores - lax.optimization_barrier(jnp.max(scores, axis=-1, keepdims=True)))
    probs = low(weights / lax.optimization_barrier(jnp.sum(weights, axis=-1, keepdims=True)))
    attended = jnp.einsum('hqk,khd->qhd', probs, value_wide, precision=HIGHEST).reshape(count, H * HD)
    attended = low(low_back(attended))
    middle = inputs + low_back(matmul(attended, w_output))
    normed_mid = low(normalize(middle, norm_mid_gain))
    gate_value = low_back(matmul(normed_mid, w_gate))
    up_value = low_back(matmul(normed_mid, w_up))
    hidden = low(gate_value * jax.nn.sigmoid(gate_value) * up_value)
    return middle + low_back(matmul(hidden, w_down))

def reference(tokens, segment_ids, positions, norm_in_gain, w_query, w_key, w_value, query_gain, key_gain, w_output, norm_mid_gain, w_gate, w_up, w_down, grad_out):
    params = tuple((item.astype(jnp.float32) for item in (norm_in_gain, w_query, w_key, w_value, query_gain, key_gain, w_output, norm_mid_gain, w_gate, w_up, w_down)))
    inputs = tokens.astype(jnp.float32).reshape(SEQS, SEQ, D)

    def forward(values, *weights):

        def single(items):
            return one_sequence(items[0], items[1], items[2], *weights)
        return lax.map(jax.checkpoint(single), (values, segment_ids, positions))
    result, pull = jax.vjp(forward, inputs, *params)
    grads = pull(grad_out.astype(jnp.float32).reshape(SEQS, SEQ, D))
    return (result.reshape(TOKENS, D).astype(jnp.bfloat16), grads[0].reshape(TOKENS, D).astype(jnp.bfloat16), grads[1], grads[2], grads[3], grads[4], grads[5], grads[6], grads[7], grads[8], grads[9], grads[10], grads[11])
```

```python
import jax
import jax.numpy as jnp
from jax import lax
from jax.sharding import PartitionSpec as P

EPSILON = 1e-05
AXES = ("dp", "tensor")
LOW = jnp.bfloat16
FULL = jnp.float32
LANES = 128


def matmul(left, right):
    return jnp.dot(left, right, preferred_element_type=FULL)


def matmul_back(left, right):
    return lax.dot_general(left, right, (((1,), (1,)), ((), ())), preferred_element_type=FULL)


def matmul_rows(left, right):
    return lax.dot_general(left, right, (((0,), (0,)), ((), ())), preferred_element_type=FULL)


def scale_of(values):
    return lax.rsqrt(jnp.mean(values * values, axis=-1, keepdims=True) + EPSILON)


def normalize(values, gain):
    return values * scale_of(values) * gain


def normalize_back(values, gain, grad):
    scale = scale_of(values)
    grad = grad * gain
    inner = jnp.mean(grad * values, axis=-1, keepdims=True)
    return scale * grad - values * (scale * scale * scale * inner)


def angles_of(places, width):
    half = width // 2
    steps = jnp.arange(half, dtype=FULL) * (2.0 / width)
    freqs = jnp.power(jnp.float32(1000000.0), -steps)
    angles = places.astype(FULL)[:, None] * freqs[None, :]
    return jnp.cos(angles)[:, None, :], jnp.sin(angles)[:, None, :]


def rotate(values, cosine, sine):
    half = values.shape[-1] // 2
    first = values[..., :half]
    second = values[..., half:]
    return jnp.concatenate(
        [first * cosine - second * sine, second * cosine + first * sine], axis=-1
    )


def pick(array, index, axis):
    return lax.dynamic_index_in_dim(array, index, axis, keepdims=False)


def ordered(mine, other, bit, axis):
    first = bit == 0
    return jnp.stack([jnp.where(first, mine, other), jnp.where(first, other, mine)], axis=axis)


class Plan:
    def __init__(self, mesh):
        self.dp = mesh.shape["dp"]
        self.tensor = mesh.shape["tensor"]
        self.devices = self.dp * self.tensor
        self.lines = self.dp // 2
        self.stride = 2 * self.tensor
        self.core_mask = 1
        self.row_mask = self.tensor // 2
        self.pair_mask = self.tensor

    def here(self):
        dp = lax.axis_index("dp")
        tensor = lax.axis_index("tensor")
        self.line = dp // 2
        self.pair = dp % 2
        self.row = tensor // 2
        self.core = tensor % 2

    def swap(self, array, mask):
        return lax.ppermute(array, AXES, [(i, i ^ mask) for i in range(self.devices)])

    def shift(self, array, step, senders):
        pairs = [
            (i, i + step * self.stride) for i in range(self.devices) if i // self.stride in senders
        ]
        return lax.ppermute(array, AXES, pairs)

    def groups(self):
        return [
            [line * 2 + pair for line in range(self.lines)] for pair in range(2)
        ]

    def gather_lines(self, array):
        count = self.lines
        if count > 4:
            return lax.all_gather(array, "dp", axis=0, axis_index_groups=self.groups())
        from_left, from_right = {}, {}
        moving_right = moving_left = array
        for step in range(1, count):
            moving_right = self.shift(moving_right, 1, range(step - 1, count - 1))
            moving_left = self.shift(moving_left, -1, range(1, count - step + 1))
            from_left[step] = moving_right
            from_right[step] = moving_left
        whole = lax.dynamic_update_index_in_dim(
            jnp.zeros((count,) + array.shape, array.dtype), array, self.line, 0
        )
        for step in range(1, count):
            value = jnp.where(self.line + step < count, from_right[step], from_left[count - step])
            whole = lax.dynamic_update_index_in_dim(whole, value, (self.line + step) % count, 0)
        return whole

    def sum_lines(self, parts):
        count = self.lines
        if count > 4:
            return lax.psum_scatter(
                parts, "dp", scatter_dimension=0, axis_index_groups=self.groups()
            ).astype(FULL)
        total = pick(parts, self.line, 0).astype(FULL)
        for sign in (1, -1):
            held = None
            for away in range(count - 1, 0, -1):
                part = pick(parts, (self.line + sign * away) % count, 0)
                if held is not None:
                    part = (part.astype(FULL) + held.astype(FULL)).astype(LOW)
                senders = range(0, count - away) if sign > 0 else range(away, count)
                held = self.shift(part, sign, senders)
            total = total + held.astype(FULL)
        return total

    def gather_rows(self, array):
        array = ordered(array, self.swap(array, self.row_mask), self.row, 0)
        array = ordered(array, self.swap(array, self.core_mask), self.core, 1)
        return array.reshape((-1,) + array.shape[3:])

    def gather_group(self, array):
        array = ordered(array, self.swap(array, self.row_mask), self.row, 0)
        array = ordered(array, self.swap(array, self.pair_mask), self.pair, 0)
        array = ordered(array, self.swap(array, self.core_mask), self.core, 2)
        return array.reshape((-1,) + array.shape[4:])

    def halve(self, array, mask, bit, axis):
        other = self.swap(pick(array, 1 - bit, axis).astype(LOW), mask)
        return pick(array, bit, axis).astype(FULL) + other.astype(FULL)

    def scatter_rows(self, array):
        array = array.reshape((2, 2, -1) + array.shape[1:])
        array = self.halve(array, self.core_mask, self.core, 1)
        return self.halve(array, self.row_mask, self.row, 0)

    def scatter_group(self, array):
        array = array.reshape((2, 2, 2, -1) + array.shape[1:])
        array = self.halve(array, self.core_mask, self.core, 2)
        array = self.halve(array, self.row_mask, self.row, 1)
        return self.halve(array, self.pair_mask, self.pair, 0)

    def own_rows(self, array):
        array = array.reshape((2, 2, 2, -1) + array.shape[1:])
        return pick(pick(pick(array, self.pair, 0), self.row, 0), self.core, 0)

    def sum_all(self, array):
        mask = 1
        while mask < self.devices:
            array = array + self.swap(array, mask)
            mask *= 2
        return array


def wide_of(columns):
    half = columns // 2
    return -(-half // LANES) * LANES


def channel_part(weight, owner):
    columns = weight.shape[1]
    half, wide = columns // 2, wide_of(columns)
    offset = columns - wide
    window = jnp.where(owner == 0, weight[:, :wide], weight[:, offset:])
    place = lax.broadcasted_iota(jnp.int32, window.shape, 1) + jnp.where(owner == 0, 0, offset)
    return jnp.where((place < half) == (owner == 0), window, jnp.zeros_like(window))


def gather_channels(plan, weight):
    other = plan.swap(channel_part(weight, 1 - plan.pair), plan.pair_mask)
    both = ordered(channel_part(weight, plan.pair), other, plan.pair, 0)
    both = both.reshape((-1, both.shape[-1]))
    return plan.gather_lines(both).reshape((-1, both.shape[-1]))


def scatter_channels(plan, grad, columns):
    grad = grad.astype(LOW)
    wide = grad.shape[1]
    summed = plan.sum_lines(grad.reshape((plan.lines, -1, wide)))
    summed = summed.reshape((2, -1, wide))
    other = plan.swap(pick(summed, 1 - plan.pair, 0).astype(LOW), plan.pair_mask).astype(FULL)
    mine = pick(summed, plan.pair, 0)
    low = jnp.where(plan.pair == 0, mine, other)
    high = jnp.where(plan.pair == 0, other, mine)
    offset = columns - wide
    return jnp.concatenate(
        [low[:, :offset], low[:, offset:] + high[:, : wide - offset], high[:, wide - offset :]],
        axis=1,
    )


def gather_model(plan, weight):
    lines = plan.gather_lines(weight)
    both = ordered(lines, plan.swap(lines, plan.pair_mask), plan.pair, 1)
    return both.reshape((-1, both.shape[-1]))


def scatter_model(plan, grad):
    grad = grad.astype(LOW).reshape((plan.lines, 2, -1, grad.shape[1]))
    grad = plan.halve(grad, plan.pair_mask, plan.pair, 1).astype(LOW)
    return plan.sum_lines(grad)


def body(
    plan,
    tokens,
    segment_ids,
    positions,
    norm_in_gain,
    w_query,
    w_key,
    w_value,
    query_gain,
    key_gain,
    w_output,
    norm_mid_gain,
    w_gate,
    w_up,
    w_down,
    grad_out,
):
    plan.here()
    head_dim = query_gain.shape[0]
    scaling = head_dim ** (-0.5)
    sequences, length = segment_ids.shape
    rows = sequences * length
    q_columns, k_columns = w_query.shape[1], w_key.shape[1]
    heads = q_columns // head_dim
    groups = k_columns // head_dim
    repeat = heads // groups
    channels = w_gate.shape[1]

    qkv_full = gather_model(plan, jnp.concatenate([w_query, w_key, w_value], axis=1))
    tokens_seq = plan.gather_rows(tokens)
    output_own = gather_model(plan, w_output.T)
    gate_full = gather_channels(plan, w_gate)
    up_full = gather_channels(plan, w_up)
    down_full = gather_channels(plan, w_down.T)
    tokens_group = ordered(
        tokens_seq, plan.swap(tokens_seq, plan.pair_mask), plan.pair, 0
    ).reshape((2 * rows, -1))
    back_group = plan.gather_group(grad_out)
    output_all = jnp.concatenate([output_own, plan.swap(output_own, plan.row_mask)], axis=1)
    output_all = jnp.concatenate([output_all, plan.swap(output_all, plan.core_mask)], axis=1)

    inputs = tokens_seq.astype(FULL)
    scaled_in = inputs * scale_of(inputs)
    rows_in = (scaled_in * norm_in_gain).astype(LOW)
    qkv = matmul(rows_in, qkv_full)
    query_raw = qkv[:, :q_columns]
    key_raw = qkv[:, q_columns : q_columns + k_columns]
    value_low = qkv[:, q_columns + k_columns :].astype(LOW)
    cosine, sine = angles_of(positions.reshape(rows), head_dim)

    def heads_local(query_in, key_in, query_scale, key_scale):
        query_out = rotate(
            normalize(query_in.reshape(rows, heads, head_dim), query_scale), cosine, sine
        )
        key_out = rotate(normalize(key_in.reshape(rows, groups, head_dim), key_scale), cosine, sine)
        return (query_out, key_out)

    (query_rot, key_rot), pull_heads = jax.vjp(
        heads_local, query_raw, key_raw, query_gain, key_gain
    )
    query_low = query_rot.astype(LOW).reshape(sequences, length, groups, repeat, head_dim)
    key_low = key_rot.astype(LOW).reshape(sequences, length, groups, head_dim)
    value_seq = value_low.reshape(sequences, length, groups, head_dim)

    def forward_one(query, key, value, segment):
        scores = (
            jnp.einsum("qgrd,kgd->grqk", query, key, preferred_element_type=FULL) * scaling
        )
        index = jnp.arange(length)
        allowed = (segment[:, None] == segment[None, :]) & (index[None, :] <= index[:, None])
        scores = jnp.where(allowed, scores, -1e30)
        weights = jnp.exp(scores - jnp.max(scores, axis=-1, keepdims=True))
        probs = weights / jnp.sum(weights, axis=-1, keepdims=True)
        result = jnp.einsum("grqk,kgd->qgrd", probs.astype(LOW), value, preferred_element_type=FULL)
        return (result, probs)

    attended, probs_all = jax.vmap(forward_one)(query_low, key_low, value_seq, segment_ids)
    attended_low = attended.reshape(rows, heads * head_dim).astype(LOW)
    attended_row = jnp.concatenate(
        [attended_low, plan.swap(attended_low, plan.row_mask)], axis=1
    )
    attended_pair = ordered(
        attended_row, plan.swap(attended_row, plan.pair_mask), plan.pair, 0
    ).reshape((2 * rows, -1))
    attended_group = jnp.concatenate(
        [attended_pair, plan.swap(attended_pair, plan.core_mask)], axis=1
    )

    middle = tokens_group.astype(FULL) + matmul_back(attended_group, output_all)
    scaled_mid = middle * scale_of(middle)
    rows_mid = (scaled_mid * norm_mid_gain).astype(LOW)
    gate_value = matmul(rows_mid, gate_full)
    up_value = matmul(rows_mid, up_full)
    logistic = jax.nn.sigmoid(gate_value)
    swish = gate_value * logistic
    hidden_low = (swish * up_value).astype(LOW)
    grad_down = matmul_rows(back_group, hidden_low)
    summed_down = scatter_channels(plan, grad_down, channels).T
    grad_hidden = matmul(back_group, down_full)
    grad_gate_low = (
        grad_hidden * up_value * logistic * (1.0 + gate_value * (1.0 - logistic))
    ).astype(LOW)
    grad_up_low = (grad_hidden * swish).astype(LOW)
    mid_part = matmul_back(grad_gate_low, gate_full) + matmul_back(grad_up_low, up_full)
    gain_mid = jnp.sum(mid_part * scaled_mid, axis=0)
    grad_normed_mid = plan.scatter_group(mid_part.astype(LOW))
    middle_own = plan.own_rows(middle)
    upstream = grad_out.astype(FULL)
    grad_middle = upstream + normalize_back(middle_own, norm_mid_gain, grad_normed_mid)
    rows_attn_back = plan.gather_rows(grad_middle.astype(LOW))

    summed_gate = scatter_channels(plan, matmul_rows(rows_mid, grad_gate_low), channels)
    summed_up = scatter_channels(plan, matmul_rows(rows_mid, grad_up_low), channels)
    mlp_part = plan.scatter_group(matmul_back(hidden_low, down_full).astype(LOW))
    block_out = (middle_own + mlp_part).astype(LOW)

    grad_attended = matmul(rows_attn_back, output_own).astype(LOW)
    grad_output = matmul_rows(rows_attn_back, attended_low)
    summed_output = scatter_model(plan, grad_output).T

    def backward_one(query, key, value, probs, grad_result):
        grad_probs = jnp.einsum("qgrd,kgd->grqk", grad_result, value, preferred_element_type=FULL)
        inner = jnp.sum(probs * grad_probs, axis=-1, keepdims=True)
        grad_scores = (probs * (grad_probs - inner)).astype(LOW)
        grad_query = (
            jnp.einsum("grqk,kgd->qgrd", grad_scores, key, preferred_element_type=FULL) * scaling
        )
        grad_key = (
            jnp.einsum("grqk,qgrd->kgd", grad_scores, query, preferred_element_type=FULL) * scaling
        )
        grad_value = jnp.einsum(
            "grqk,qgrd->kgd", probs.astype(LOW), grad_result, preferred_element_type=FULL
        )
        return (grad_query, grad_key, grad_value)

    grad_heads = grad_attended.reshape(sequences, length, groups, repeat, head_dim)
    grad_query_all, grad_key_all, grad_value_all = jax.vmap(backward_one)(
        query_low, key_low, value_seq, probs_all, grad_heads
    )
    grad_query_raw, grad_key_raw, grad_query_scale, grad_key_scale = pull_heads(
        (
            grad_query_all.reshape(rows, heads, head_dim),
            grad_key_all.reshape(rows, groups, head_dim),
        )
    )
    grad_qkv = jnp.concatenate(
        [
            grad_query_raw.astype(LOW),
            grad_key_raw.astype(LOW),
            grad_value_all.reshape(rows, k_columns).astype(LOW),
        ],
        axis=1,
    )
    summed_qkv = scatter_model(plan, matmul_rows(rows_in, grad_qkv))
    in_part = matmul_back(grad_qkv, qkv_full)
    gain_in = jnp.sum(in_part * scaled_in, axis=0)
    grad_normed_in = plan.scatter_rows(in_part.astype(LOW))
    grad_tokens = (
        grad_middle + normalize_back(tokens.astype(FULL), norm_in_gain, grad_normed_in)
    ).astype(LOW)

    gains = plan.sum_all(
        jnp.concatenate([gain_in, gain_mid, grad_query_scale, grad_key_scale])
    )
    width = gain_in.shape[0]
    return (
        block_out,
        grad_tokens,
        gains[:width],
        summed_qkv[:, :q_columns],
        summed_qkv[:, q_columns : q_columns + k_columns],
        summed_qkv[:, q_columns + k_columns :],
        gains[2 * width : 2 * width + head_dim],
        gains[2 * width + head_dim :],
        summed_output,
        gains[width : 2 * width],
        summed_gate,
        summed_up,
        summed_down,
    )


def solution(mesh):
    plan = Plan(mesh)

    def step(*args):
        return body(plan, *args)

    return jax.shard_map(
        step,
        mesh=mesh,
        in_specs=(
            P(("dp", "tensor"), None),
            P("dp", None),
            P("dp", None),
            P(),
            P("dp", "tensor"),
            P("dp", "tensor"),
            P("dp", "tensor"),
            P(),
            P(),
            P("tensor", "dp"),
            P(),
            P("dp", "tensor"),
            P("dp", "tensor"),
            P("tensor", "dp"),
            P(("dp", "tensor"), None),
        ),
        out_specs=(
            P(("dp", "tensor"), None),
            P(("dp", "tensor"), None),
            P(),
            P("dp", "tensor"),
            P("dp", "tensor"),
            P("dp", "tensor"),
            P(),
            P(),
            P("tensor", "dp"),
            P(),
            P("dp", "tensor"),
            P("dp", "tensor"),
            P("tensor", "dp"),
        ),
        check_vma=False,
    )
```

```python
import jax
import jax.numpy as jnp
from jax import lax
from jax.sharding import PartitionSpec as P

EPSILON = 1e-05
AXES = ("dp", "tensor")
LOW = jnp.bfloat16
FULL = jnp.float32
LANES = 128


def matmul(left, right):
    return jnp.dot(left, right, preferred_element_type=FULL)


def matmul_back(left, right):
    return lax.dot_general(left, right, (((1,), (1,)), ((), ())), preferred_element_type=FULL)


def matmul_rows(left, right):
    return lax.dot_general(left, right, (((0,), (0,)), ((), ())), preferred_element_type=FULL)


def scale_of(values):
    return lax.rsqrt(jnp.mean(values * values, axis=-1, keepdims=True) + EPSILON)


def normalize(values, gain):
    return values * scale_of(values) * gain


def normalize_back(values, gain, grad):
    scale = scale_of(values)
    grad = grad * gain
    inner = jnp.mean(grad * values, axis=-1, keepdims=True)
    return scale * grad - values * (scale * scale * scale * inner)


def angles_of(places, width):
    half = width // 2
    steps = jnp.arange(half, dtype=FULL) * (2.0 / width)
    freqs = jnp.power(jnp.float32(1000000.0), -steps)
    angles = places.astype(FULL)[:, None] * freqs[None, :]
    return jnp.cos(angles)[:, None, :], jnp.sin(angles)[:, None, :]


def rotate(values, cosine, sine):
    half = values.shape[-1] // 2
    first = values[..., :half]
    second = values[..., half:]
    return jnp.concatenate(
        [first * cosine - second * sine, second * cosine + first * sine], axis=-1
    )


def pick(array, index, axis):
    return lax.dynamic_index_in_dim(array, index, axis, keepdims=False)


def ordered(mine, other, bit, axis):
    first = bit == 0
    return jnp.stack([jnp.where(first, mine, other), jnp.where(first, other, mine)], axis=axis)


class Plan:
    def __init__(self, mesh):
        self.dp = mesh.shape["dp"]
        self.tensor = mesh.shape["tensor"]
        self.devices = self.dp * self.tensor
        self.lines = self.dp // 2
        self.stride = 2 * self.tensor
        self.core_mask = 1
        self.row_mask = self.tensor // 2
        self.pair_mask = self.tensor

    def here(self):
        dp = lax.axis_index("dp")
        tensor = lax.axis_index("tensor")
        self.line = dp // 2
        self.pair = dp % 2
        self.row = tensor // 2
        self.core = tensor % 2

    def swap(self, array, mask):
        return lax.ppermute(array, AXES, [(i, i ^ mask) for i in range(self.devices)])

    def groups(self):
        return [
            [line * 2 + pair for line in range(self.lines)] for pair in range(2)
        ]

    def gather_lines(self, array):
        return lax.all_gather(array, "dp", axis=0, tiled=True, axis_index_groups=self.groups())

    def sum_lines(self, parts):
        return lax.psum_scatter(
            parts, "dp", scatter_dimension=0, tiled=True, axis_index_groups=self.groups()
        )

    def gather_lines_direct(self, array):
        count = self.lines
        if count > 4:
            return lax.all_gather(array, "dp", axis=0, axis_index_groups=self.groups())
        whole = lax.dynamic_update_index_in_dim(
            jnp.zeros((count,) + array.shape, array.dtype), array, self.line, 0
        )
        others = [self.swap(array, away * self.stride) for away in range(1, count)]
        for away, other in enumerate(others, 1):
            whole = lax.dynamic_update_index_in_dim(whole, other, self.line ^ away, 0)
        return whole

    def sum_lines_direct(self, parts):
        count = self.lines
        if count > 4:
            return lax.psum_scatter(
                parts, "dp", scatter_dimension=0, axis_index_groups=self.groups()
            ).astype(FULL)
        others = [
            self.swap(pick(parts, self.line ^ away, 0), away * self.stride)
            for away in range(1, count)
        ]
        return sum([other.astype(FULL) for other in others], pick(parts, self.line, 0).astype(FULL))

    def gather_rows(self, array):
        array = ordered(array, self.swap(array, self.row_mask), self.row, 0)
        array = ordered(array, self.swap(array, self.core_mask), self.core, 1)
        return array.reshape((-1,) + array.shape[3:])

    def gather_group(self, array):
        row, pair, both = [
            self.swap(array, mask)
            for mask in (self.row_mask, self.pair_mask, self.row_mask | self.pair_mask)
        ]
        array = ordered(
            ordered(array, row, self.row, 0), ordered(pair, both, self.row, 0), self.pair, 0
        )
        array = ordered(array, self.swap(array, self.core_mask), self.core, 2)
        return array.reshape((-1,) + array.shape[4:])

    def halve(self, array, mask, bit, axis):
        other = self.swap(pick(array, 1 - bit, axis).astype(LOW), mask)
        return pick(array, bit, axis).astype(FULL) + other.astype(FULL)

    def scatter_rows(self, array):
        array = array.reshape((2, 2, -1) + array.shape[1:])
        array = self.halve(array, self.core_mask, self.core, 1)
        return self.halve(array, self.row_mask, self.row, 0)

    def scatter_group(self, array):
        array = array.reshape((2, 2, 2, -1) + array.shape[1:])
        array = self.halve(array, self.core_mask, self.core, 2).astype(LOW)

        def part(pair, row):
            return pick(pick(array, pair, 0), row, 0)

        others = [
            self.swap(part(1 - self.pair, 1 - self.row), self.pair_mask | self.row_mask),
            self.swap(part(1 - self.pair, self.row), self.pair_mask),
            self.swap(part(self.pair, 1 - self.row), self.row_mask),
        ]
        return sum([other.astype(FULL) for other in others], part(self.pair, self.row).astype(FULL))

    def sum_all(self, array):
        mask = 1
        while mask < self.devices:
            array = array + self.swap(array, mask)
            mask *= 2
        return array


def wide_of(columns):
    half = columns // 2
    return -(-half // LANES) * LANES


def channel_part(weight, owner):
    columns = weight.shape[1]
    half, wide = columns // 2, wide_of(columns)
    offset = columns - wide
    window = jnp.where(owner == 0, weight[:, :wide], weight[:, offset:])
    place = lax.broadcasted_iota(jnp.int32, window.shape, 1) + jnp.where(owner == 0, 0, offset)
    return jnp.where((place < half) == (owner == 0), window, jnp.zeros_like(window))


def spread_channels(plan, weights):
    mine, theirs = [
        jnp.concatenate([channel_part(weight, owner) for weight in weights], axis=1)
        for owner in (plan.pair, 1 - plan.pair)
    ]
    both = ordered(mine, plan.swap(theirs, plan.pair_mask), plan.pair, 0)
    return both.reshape((-1, both.shape[-1]))


def collect_channels(plan, summed, columns):
    wide = wide_of(columns)
    summed = summed.reshape((2, -1, summed.shape[1]))
    other = plan.swap(pick(summed, 1 - plan.pair, 0), plan.pair_mask).astype(FULL)
    mine = pick(summed, plan.pair, 0).astype(FULL)
    first = jnp.where(plan.pair == 0, mine, other)
    second = jnp.where(plan.pair == 0, other, mine)
    offset = columns - wide
    results = []
    for start in range(0, summed.shape[2], wide):
        low, high = first[:, start : start + wide], second[:, start : start + wide]
        results.append(
            jnp.concatenate(
                [
                    low[:, :offset],
                    low[:, offset:] + high[:, : wide - offset],
                    high[:, wide - offset :],
                ],
                axis=1,
            )
        )
    return results


def gather_model(plan, weight):
    lines = plan.gather_lines_direct(weight)
    both = ordered(lines, plan.swap(lines, plan.pair_mask), plan.pair, 1)
    return both.reshape((-1, both.shape[-1]))


def scatter_model(plan, grad):
    grad = grad.astype(LOW).reshape((plan.lines, 2, -1, grad.shape[1]))
    grad = plan.halve(grad, plan.pair_mask, plan.pair, 1).astype(LOW)
    return plan.sum_lines_direct(grad)


def body(
    plan,
    tokens,
    segment_ids,
    positions,
    norm_in_gain,
    w_query,
    w_key,
    w_value,
    query_gain,
    key_gain,
    w_output,
    norm_mid_gain,
    w_gate,
    w_up,
    w_down,
    grad_out,
):
    plan.here()
    head_dim = query_gain.shape[0]
    scaling = head_dim ** (-0.5)
    sequences, length = segment_ids.shape
    rows = sequences * length
    q_columns, k_columns = w_query.shape[1], w_key.shape[1]
    heads = q_columns // head_dim
    groups = k_columns // head_dim
    repeat = heads // groups
    channels = w_gate.shape[1]

    qkv_columns = q_columns + 2 * k_columns
    wide = wide_of(channels)

    model_full = gather_model(
        plan, jnp.concatenate([w_query, w_key, w_value, w_output.T], axis=1)
    )
    qkv_full = model_full[:, :qkv_columns]
    output_own = model_full[:, qkv_columns:]
    tokens_seq = plan.gather_rows(tokens)
    windows = spread_channels(plan, [w_gate, w_up, w_down.T])
    gate_up_full = plan.gather_lines(windows[:, : 2 * wide])
    down_full = plan.gather_lines(windows[:, 2 * wide :])
    back_group = plan.gather_group(grad_out)

    inputs = tokens_seq.astype(FULL)
    scaled_in = inputs * scale_of(inputs)
    rows_in = (scaled_in * norm_in_gain).astype(LOW)
    qkv = matmul(rows_in, qkv_full)
    query_raw = qkv[:, :q_columns]
    key_raw = qkv[:, q_columns : q_columns + k_columns]
    value_low = qkv[:, q_columns + k_columns :].astype(LOW)
    cosine, sine = angles_of(positions.reshape(rows), head_dim)

    def heads_local(query_in, key_in, query_scale, key_scale):
        query_out = rotate(
            normalize(query_in.reshape(rows, heads, head_dim), query_scale), cosine, sine
        )
        key_out = rotate(normalize(key_in.reshape(rows, groups, head_dim), key_scale), cosine, sine)
        return (query_out, key_out)

    (query_rot, key_rot), pull_heads = jax.vjp(
        heads_local, query_raw, key_raw, query_gain, key_gain
    )
    query_low = query_rot.astype(LOW).reshape(sequences, length, groups, repeat, head_dim)
    key_low = key_rot.astype(LOW).reshape(sequences, length, groups, head_dim)
    value_seq = value_low.reshape(sequences, length, groups, head_dim)

    def forward_one(query, key, value, segment):
        scores = (
            jnp.einsum("qgrd,kgd->grqk", query, key, preferred_element_type=FULL) * scaling
        )
        index = jnp.arange(length)
        allowed = (segment[:, None] == segment[None, :]) & (index[None, :] <= index[:, None])
        scores = jnp.where(allowed, scores, -1e30)
        weights = jnp.exp(scores - jnp.max(scores, axis=-1, keepdims=True))
        probs = weights / jnp.sum(weights, axis=-1, keepdims=True)
        result = jnp.einsum("grqk,kgd->qgrd", probs.astype(LOW), value, preferred_element_type=FULL)
        return (result, probs)

    attended, probs_all = jax.vmap(forward_one)(query_low, key_low, value_seq, segment_ids)
    attended_low = attended.reshape(rows, heads * head_dim).astype(LOW)
    attn_part = plan.scatter_rows(matmul_back(attended_low, output_own).astype(LOW))

    middle = tokens.astype(FULL) + attn_part
    scaled_mid = middle * scale_of(middle)
    rows_mid = plan.gather_group((scaled_mid * norm_mid_gain).astype(LOW))
    gate_up = matmul(rows_mid, gate_up_full)
    gate_value, up_value = gate_up[:, :wide], gate_up[:, wide:]
    logistic = jax.nn.sigmoid(gate_value)
    swish = gate_value * logistic
    hidden_low = (swish * up_value).astype(LOW)
    down_sum = plan.sum_lines(matmul_rows(back_group, hidden_low).astype(LOW))
    grad_hidden = matmul(back_group, down_full)
    grad_gate_low = (
        grad_hidden * up_value * logistic * (1.0 + gate_value * (1.0 - logistic))
    ).astype(LOW)
    grad_up_low = (grad_hidden * swish).astype(LOW)
    grad_gate_up = jnp.concatenate([grad_gate_low, grad_up_low], axis=1)
    grad_normed_mid = plan.scatter_group(matmul_back(grad_gate_up, gate_up_full).astype(LOW))
    gain_mid = jnp.sum(grad_normed_mid * scaled_mid, axis=0)
    upstream = grad_out.astype(FULL)
    grad_middle = upstream + normalize_back(middle, norm_mid_gain, grad_normed_mid)
    rows_attn_back = plan.gather_rows(grad_middle.astype(LOW))

    gate_up_sum = plan.sum_lines(matmul_rows(rows_mid, grad_gate_up).astype(LOW))
    mlp_part = plan.scatter_group(matmul_back(hidden_low, down_full).astype(LOW))
    block_out = (middle + mlp_part).astype(LOW)
    (summed_down,) = collect_channels(plan, down_sum, channels)
    summed_gate, summed_up = collect_channels(plan, gate_up_sum, channels)

    grad_attended = matmul(rows_attn_back, output_own).astype(LOW)
    grad_output = matmul_rows(rows_attn_back, attended_low).astype(LOW)

    def backward_one(query, key, value, probs, grad_result):
        grad_probs = jnp.einsum("qgrd,kgd->grqk", grad_result, value, preferred_element_type=FULL)
        inner = jnp.sum(probs * grad_probs, axis=-1, keepdims=True)
        grad_scores = (probs * (grad_probs - inner)).astype(LOW)
        grad_query = (
            jnp.einsum("grqk,kgd->qgrd", grad_scores, key, preferred_element_type=FULL) * scaling
        )
        grad_key = (
            jnp.einsum("grqk,qgrd->kgd", grad_scores, query, preferred_element_type=FULL) * scaling
        )
        grad_value = jnp.einsum(
            "grqk,qgrd->kgd", probs.astype(LOW), grad_result, preferred_element_type=FULL
        )
        return (grad_query, grad_key, grad_value)

    grad_heads = grad_attended.reshape(sequences, length, groups, repeat, head_dim)
    grad_query_all, grad_key_all, grad_value_all = jax.vmap(backward_one)(
        query_low, key_low, value_seq, probs_all, grad_heads
    )
    grad_query_raw, grad_key_raw, grad_query_scale, grad_key_scale = pull_heads(
        (
            grad_query_all.reshape(rows, heads, head_dim),
            grad_key_all.reshape(rows, groups, head_dim),
        )
    )
    grad_qkv = jnp.concatenate(
        [
            grad_query_raw.astype(LOW),
            grad_key_raw.astype(LOW),
            grad_value_all.reshape(rows, k_columns).astype(LOW),
        ],
        axis=1,
    )
    summed_model = scatter_model(
        plan,
        jnp.concatenate([matmul_rows(rows_in, grad_qkv).astype(LOW), grad_output], axis=1),
    )
    in_part = matmul_back(grad_qkv, qkv_full)
    gain_in = jnp.sum(in_part * scaled_in, axis=0)
    grad_normed_in = plan.scatter_rows(in_part.astype(LOW))
    grad_tokens = (
        grad_middle + normalize_back(tokens.astype(FULL), norm_in_gain, grad_normed_in)
    ).astype(LOW)

    gains = plan.sum_all(
        jnp.concatenate([gain_in, gain_mid, grad_query_scale, grad_key_scale])
    )
    width = gain_in.shape[0]
    return (
        block_out,
        grad_tokens,
        gains[:width],
        summed_model[:, :q_columns],
        summed_model[:, q_columns : q_columns + k_columns],
        summed_model[:, q_columns + k_columns : qkv_columns],
        gains[2 * width : 2 * width + head_dim],
        gains[2 * width + head_dim :],
        summed_model[:, qkv_columns:].T,
        gains[width : 2 * width],
        summed_gate,
        summed_up,
        summed_down.T,
    )


def solution(mesh):
    plan = Plan(mesh)

    def step(*args):
        return body(plan, *args)

    return jax.shard_map(
        step,
        mesh=mesh,
        in_specs=(
            P(("dp", "tensor"), None),
            P("dp", None),
            P("dp", None),
            P(),
            P("dp", "tensor"),
            P("dp", "tensor"),
            P("dp", "tensor"),
            P(),
            P(),
            P("tensor", "dp"),
            P(),
            P("dp", "tensor"),
            P("dp", "tensor"),
            P("tensor", "dp"),
            P(("dp", "tensor"), None),
        ),
        out_specs=(
            P(("dp", "tensor"), None),
            P(("dp", "tensor"), None),
            P(),
            P("dp", "tensor"),
            P("dp", "tensor"),
            P("dp", "tensor"),
            P(),
            P(),
            P("tensor", "dp"),
            P(),
            P("dp", "tensor"),
            P("dp", "tensor"),
            P("tensor", "dp"),
        ),
        check_vma=False,
    )
```

```python
import jax
import jax.numpy as jnp
from jax import lax
from jax.sharding import PartitionSpec as P

EPSILON = 1e-05
AXES = ("dp", "tensor")
LOW = jnp.bfloat16
FULL = jnp.float32
LANES = 128


def matmul(left, right):
    return jnp.dot(left, right, preferred_element_type=FULL)


def matmul_back(left, right):
    return lax.dot_general(left, right, (((1,), (1,)), ((), ())), preferred_element_type=FULL)


def matmul_rows(left, right):
    return lax.dot_general(left, right, (((0,), (0,)), ((), ())), preferred_element_type=FULL)


def scale_of(values):
    return lax.rsqrt(jnp.mean(values * values, axis=-1, keepdims=True) + EPSILON)


def normalize(values, gain):
    return values * scale_of(values) * gain


def normalize_back(values, gain, grad):
    scale = scale_of(values)
    grad = grad * gain
    inner = jnp.mean(grad * values, axis=-1, keepdims=True)
    return scale * grad - values * (scale * scale * scale * inner)


def angles_of(places, width):
    half = width // 2
    steps = jnp.arange(half, dtype=FULL) * (2.0 / width)
    freqs = jnp.power(jnp.float32(1000000.0), -steps)
    angles = places.astype(FULL)[:, None] * freqs[None, :]
    return jnp.cos(angles)[:, None, :], jnp.sin(angles)[:, None, :]


def rotate(values, cosine, sine):
    half = values.shape[-1] // 2
    first = values[..., :half]
    second = values[..., half:]
    return jnp.concatenate(
        [first * cosine - second * sine, second * cosine + first * sine], axis=-1
    )


def pick(array, index, axis):
    return lax.dynamic_index_in_dim(array, index, axis, keepdims=False)


def ordered(mine, other, bit, axis):
    first = bit == 0
    return jnp.stack([jnp.where(first, mine, other), jnp.where(first, other, mine)], axis=axis)


def after(array, *others):
    return lax.optimization_barrier((array,) + others)[0]


class Plan:
    def __init__(self, mesh):
        self.dp = mesh.shape["dp"]
        self.tensor = mesh.shape["tensor"]
        self.devices = self.dp * self.tensor
        self.lines = self.dp // 2
        self.stride = 2 * self.tensor
        self.core_mask = 1
        self.row_mask = self.tensor // 2
        self.pair_mask = self.tensor

    def here(self):
        dp = lax.axis_index("dp")
        tensor = lax.axis_index("tensor")
        self.line = dp // 2
        self.pair = dp % 2
        self.row = tensor // 2
        self.core = tensor % 2

    def swap(self, array, mask):
        return lax.ppermute(array, AXES, [(i, i ^ mask) for i in range(self.devices)])

    def groups(self):
        return [
            [line * 2 + pair for line in range(self.lines)] for pair in range(2)
        ]

    def gather_lines(self, array):
        return lax.all_gather(array, "dp", axis=0, tiled=True, axis_index_groups=self.groups())

    def sum_lines(self, parts):
        return lax.psum_scatter(
            parts, "dp", scatter_dimension=0, tiled=True, axis_index_groups=self.groups()
        )

    def gather_lines_direct(self, array):
        count = self.lines
        if count > 4:
            return lax.all_gather(array, "dp", axis=0, axis_index_groups=self.groups())
        whole = lax.dynamic_update_index_in_dim(
            jnp.zeros((count,) + array.shape, array.dtype), array, self.line, 0
        )
        others = [self.swap(array, away * self.stride) for away in range(1, count)]
        for away, other in enumerate(others, 1):
            whole = lax.dynamic_update_index_in_dim(whole, other, self.line ^ away, 0)
        return whole

    def sum_lines_direct(self, parts):
        count = self.lines
        if count > 4:
            return lax.psum_scatter(
                parts, "dp", scatter_dimension=0, axis_index_groups=self.groups()
            ).astype(FULL)
        others = [
            self.swap(pick(parts, self.line ^ away, 0), away * self.stride)
            for away in range(1, count)
        ]
        return sum([other.astype(FULL) for other in others], pick(parts, self.line, 0).astype(FULL))

    def gather_rows(self, array):
        array = ordered(array, self.swap(array, self.row_mask), self.row, 0)
        array = ordered(array, self.swap(array, self.core_mask), self.core, 1)
        return array.reshape((-1,) + array.shape[3:])

    def gather_group(self, array):
        row, pair, both = [
            self.swap(array, mask)
            for mask in (self.row_mask, self.pair_mask, self.row_mask | self.pair_mask)
        ]
        array = ordered(
            ordered(array, row, self.row, 0), ordered(pair, both, self.row, 0), self.pair, 0
        )
        array = ordered(array, self.swap(array, self.core_mask), self.core, 2)
        return array.reshape((-1,) + array.shape[4:])

    def halve(self, array, mask, bit, axis):
        other = self.swap(pick(array, 1 - bit, axis).astype(LOW), mask)
        return pick(array, bit, axis).astype(FULL) + other.astype(FULL)

    def scatter_rows(self, array):
        array = array.reshape((2, 2, -1) + array.shape[1:])
        array = self.halve(array, self.core_mask, self.core, 1)
        return self.halve(array, self.row_mask, self.row, 0)

    def scatter_group(self, array):
        array = array.reshape((2, 2, 2, -1) + array.shape[1:])
        array = self.halve(array, self.core_mask, self.core, 2).astype(LOW)

        def part(pair, row):
            return pick(pick(array, pair, 0), row, 0)

        others = [
            self.swap(part(1 - self.pair, 1 - self.row), self.pair_mask | self.row_mask),
            self.swap(part(1 - self.pair, self.row), self.pair_mask),
            self.swap(part(self.pair, 1 - self.row), self.row_mask),
        ]
        return sum([other.astype(FULL) for other in others], part(self.pair, self.row).astype(FULL))

    def sum_all(self, array):
        mask = 1
        while mask < self.devices:
            array = array + self.swap(array, mask)
            mask *= 2
        return array


def wide_of(columns):
    half = columns // 2
    return -(-half // LANES) * LANES


def channel_part(weight, owner):
    columns = weight.shape[1]
    half, wide = columns // 2, wide_of(columns)
    offset = columns - wide
    window = jnp.where(owner == 0, weight[:, :wide], weight[:, offset:])
    place = lax.broadcasted_iota(jnp.int32, window.shape, 1) + jnp.where(owner == 0, 0, offset)
    return jnp.where((place < half) == (owner == 0), window, jnp.zeros_like(window))


def spread_channels(plan, weights):
    mine, theirs = [
        jnp.concatenate([channel_part(weight, owner) for weight in weights], axis=1)
        for owner in (plan.pair, 1 - plan.pair)
    ]
    both = ordered(mine, plan.swap(theirs, plan.pair_mask), plan.pair, 0)
    return both.reshape((-1, both.shape[-1]))


def collect_channels(plan, summed, columns):
    wide = wide_of(columns)
    summed = summed.reshape((2, -1, summed.shape[1]))
    other = plan.swap(pick(summed, 1 - plan.pair, 0), plan.pair_mask).astype(FULL)
    mine = pick(summed, plan.pair, 0).astype(FULL)
    first = jnp.where(plan.pair == 0, mine, other)
    second = jnp.where(plan.pair == 0, other, mine)
    offset = columns - wide
    results = []
    for start in range(0, summed.shape[2], wide):
        low, high = first[:, start : start + wide], second[:, start : start + wide]
        results.append(
            jnp.concatenate(
                [
                    low[:, :offset],
                    low[:, offset:] + high[:, : wide - offset],
                    high[:, wide - offset :],
                ],
                axis=1,
            )
        )
    return results


def gather_model(plan, weight):
    lines = plan.gather_lines_direct(weight)
    both = ordered(lines, plan.swap(lines, plan.pair_mask), plan.pair, 1)
    return both.reshape((-1, both.shape[-1]))


def scatter_model(plan, grad):
    grad = grad.astype(LOW).reshape((plan.lines, 2, -1, grad.shape[1]))
    grad = plan.halve(grad, plan.pair_mask, plan.pair, 1).astype(LOW)
    return plan.sum_lines_direct(grad)


def body(
    plan,
    tokens,
    segment_ids,
    positions,
    norm_in_gain,
    w_query,
    w_key,
    w_value,
    query_gain,
    key_gain,
    w_output,
    norm_mid_gain,
    w_gate,
    w_up,
    w_down,
    grad_out,
):
    plan.here()
    head_dim = query_gain.shape[0]
    scaling = head_dim ** (-0.5)
    sequences, length = segment_ids.shape
    rows = sequences * length
    q_columns, k_columns = w_query.shape[1], w_key.shape[1]
    heads = q_columns // head_dim
    groups = k_columns // head_dim
    repeat = heads // groups
    channels = w_gate.shape[1]

    qkv_columns = q_columns + 2 * k_columns
    wide = wide_of(channels)

    model_full = gather_model(
        plan, jnp.concatenate([w_query, w_key, w_value, w_output.T], axis=1)
    )
    qkv_full = model_full[:, :qkv_columns]
    output_own = model_full[:, qkv_columns:]
    tokens_seq = plan.gather_rows(tokens)
    windows = spread_channels(plan, [w_gate, w_up, w_down.T])
    gate_up_full = plan.gather_lines(windows[:, : 2 * wide])
    down_full = plan.gather_lines(windows[:, 2 * wide :])
    back_group = plan.gather_group(grad_out)

    inputs = tokens_seq.astype(FULL)
    scaled_in = inputs * scale_of(inputs)
    rows_in = (scaled_in * norm_in_gain).astype(LOW)
    qkv = matmul(rows_in, qkv_full)
    query_raw = qkv[:, :q_columns]
    key_raw = qkv[:, q_columns : q_columns + k_columns]
    value_low = qkv[:, q_columns + k_columns :].astype(LOW)
    cosine, sine = angles_of(positions.reshape(rows), head_dim)

    def heads_local(query_in, key_in, query_scale, key_scale):
        query_out = rotate(
            normalize(query_in.reshape(rows, heads, head_dim), query_scale), cosine, sine
        )
        key_out = rotate(normalize(key_in.reshape(rows, groups, head_dim), key_scale), cosine, sine)
        return (query_out, key_out)

    (query_rot, key_rot), pull_heads = jax.vjp(
        heads_local, query_raw, key_raw, query_gain, key_gain
    )
    query_low = query_rot.astype(LOW).reshape(sequences, length, groups, repeat, head_dim)
    key_low = key_rot.astype(LOW).reshape(sequences, length, groups, head_dim)
    value_seq = value_low.reshape(sequences, length, groups, head_dim)

    def forward_one(query, key, value, segment):
        scores = (
            jnp.einsum("qgrd,kgd->grqk", query, key, preferred_element_type=FULL) * scaling
        )
        index = jnp.arange(length)
        allowed = (segment[:, None] == segment[None, :]) & (index[None, :] <= index[:, None])
        scores = jnp.where(allowed, scores, -1e30)
        weights = jnp.exp(scores - jnp.max(scores, axis=-1, keepdims=True))
        probs = weights / jnp.sum(weights, axis=-1, keepdims=True)
        result = jnp.einsum("grqk,kgd->qgrd", probs.astype(LOW), value, preferred_element_type=FULL)
        return (result, probs)

    attended, probs_all = jax.vmap(forward_one)(query_low, key_low, value_seq, segment_ids)
    attended_low = attended.reshape(rows, heads * head_dim).astype(LOW)
    attn_part = plan.scatter_rows(matmul_back(attended_low, output_own).astype(LOW))

    middle = tokens.astype(FULL) + attn_part
    scaled_mid = middle * scale_of(middle)
    rows_mid = plan.gather_group((scaled_mid * norm_mid_gain).astype(LOW))
    gate_up = matmul(rows_mid, gate_up_full)
    gate_value, up_value = gate_up[:, :wide], gate_up[:, wide:]
    logistic = jax.nn.sigmoid(gate_value)
    swish = gate_value * logistic
    hidden_low = (swish * up_value).astype(LOW)
    down_sum = plan.sum_lines(matmul_rows(back_group, hidden_low).astype(LOW))
    grad_hidden = matmul(back_group, down_full)
    grad_gate_low = (
        grad_hidden * up_value * logistic * (1.0 + gate_value * (1.0 - logistic))
    ).astype(LOW)
    grad_up_low = (grad_hidden * swish).astype(LOW)
    grad_gate_up = jnp.concatenate([grad_gate_low, grad_up_low], axis=1)
    grad_normed_mid = plan.scatter_group(matmul_back(grad_gate_up, gate_up_full).astype(LOW))
    gain_mid = jnp.sum(grad_normed_mid * scaled_mid, axis=0)
    upstream = grad_out.astype(FULL)
    grad_middle = upstream + normalize_back(middle, norm_mid_gain, grad_normed_mid)
    rows_attn_back = plan.gather_rows(grad_middle.astype(LOW))

    gate_up_sum = plan.sum_lines(matmul_rows(rows_mid, grad_gate_up).astype(LOW))
    mlp_part = plan.scatter_group(matmul_back(hidden_low, down_full).astype(LOW))
    block_out = (middle + mlp_part).astype(LOW)
    (summed_down,) = collect_channels(plan, down_sum, channels)
    summed_gate, summed_up = collect_channels(plan, gate_up_sum, channels)

    grad_attended = matmul(rows_attn_back, output_own).astype(LOW)
    summed_output = scatter_model(plan, matmul_rows(rows_attn_back, attended_low)).T

    def backward_one(query, key, value, probs, grad_result):
        grad_probs = jnp.einsum("qgrd,kgd->grqk", grad_result, value, preferred_element_type=FULL)
        inner = jnp.sum(probs * grad_probs, axis=-1, keepdims=True)
        grad_scores = (probs * (grad_probs - inner)).astype(LOW)
        grad_query = (
            jnp.einsum("grqk,kgd->qgrd", grad_scores, key, preferred_element_type=FULL) * scaling
        )
        grad_key = (
            jnp.einsum("grqk,qgrd->kgd", grad_scores, query, preferred_element_type=FULL) * scaling
        )
        grad_value = jnp.einsum(
            "grqk,qgrd->kgd", probs.astype(LOW), grad_result, preferred_element_type=FULL
        )
        return (grad_query, grad_key, grad_value)

    grad_heads = grad_attended.reshape(sequences, length, groups, repeat, head_dim)
    grad_query_all, grad_key_all, grad_value_all = jax.vmap(backward_one)(
        query_low, key_low, value_seq, probs_all, grad_heads
    )
    grad_query_raw, grad_key_raw, grad_query_scale, grad_key_scale = pull_heads(
        (
            grad_query_all.reshape(rows, heads, head_dim),
            grad_key_all.reshape(rows, groups, head_dim),
        )
    )
    grad_qkv = jnp.concatenate(
        [
            grad_query_raw.astype(LOW),
            grad_key_raw.astype(LOW),
            grad_value_all.reshape(rows, k_columns).astype(LOW),
        ],
        axis=1,
    )
    summed_model = scatter_model(plan, matmul_rows(rows_in, grad_qkv))
    in_part = matmul_back(grad_qkv, qkv_full)
    gain_in = jnp.sum(in_part * scaled_in, axis=0)
    grad_normed_in = plan.scatter_rows(in_part.astype(LOW))
    grad_tokens = (
        grad_middle + normalize_back(tokens.astype(FULL), norm_in_gain, grad_normed_in)
    ).astype(LOW)

    gains = plan.sum_all(
        jnp.concatenate([gain_in, gain_mid, grad_query_scale, grad_key_scale])
    )
    width = gain_in.shape[0]
    return (
        block_out,
        grad_tokens,
        gains[:width],
        summed_model[:, :q_columns],
        summed_model[:, q_columns : q_columns + k_columns],
        summed_model[:, q_columns + k_columns :],
        gains[2 * width : 2 * width + head_dim],
        gains[2 * width + head_dim :],
        summed_output,
        gains[width : 2 * width],
        summed_gate,
        summed_up,
        summed_down.T,
    )


def solution(mesh):
    plan = Plan(mesh)

    def step(*args):
        return body(plan, *args)

    return jax.shard_map(
        step,
        mesh=mesh,
        in_specs=(
            P(("dp", "tensor"), None),
            P("dp", None),
            P("dp", None),
            P(),
            P("dp", "tensor"),
            P("dp", "tensor"),
            P("dp", "tensor"),
            P(),
            P(),
            P("tensor", "dp"),
            P(),
            P("dp", "tensor"),
            P("dp", "tensor"),
            P("tensor", "dp"),
            P(("dp", "tensor"), None),
        ),
        out_specs=(
            P(("dp", "tensor"), None),
            P(("dp", "tensor"), None),
            P(),
            P("dp", "tensor"),
            P("dp", "tensor"),
            P("dp", "tensor"),
            P(),
            P(),
            P("tensor", "dp"),
            P(),
            P("dp", "tensor"),
            P("dp", "tensor"),
            P("tensor", "dp"),
        ),
        check_vma=False,
    )
```

```python
import jax
import jax.numpy as jnp
from jax import lax
from jax.sharding import PartitionSpec as P

EPSILON = 1e-05
AXES = ("dp", "tensor")
LOW = jnp.bfloat16
FULL = jnp.float32
LANES = 128


def matmul(left, right):
    return jnp.dot(left, right, preferred_element_type=FULL)


def matmul_back(left, right):
    return lax.dot_general(left, right, (((1,), (1,)), ((), ())), preferred_element_type=FULL)


def matmul_rows(left, right):
    return lax.dot_general(left, right, (((0,), (0,)), ((), ())), preferred_element_type=FULL)


def scale_of(values):
    return lax.rsqrt(jnp.mean(values * values, axis=-1, keepdims=True) + EPSILON)


def normalize(values, gain):
    return values * scale_of(values) * gain


def normalize_back(values, gain, grad):
    scale = scale_of(values)
    grad = grad * gain
    inner = jnp.mean(grad * values, axis=-1, keepdims=True)
    return scale * grad - values * (scale * scale * scale * inner)


def angles_of(places, width):
    half = width // 2
    steps = jnp.arange(half, dtype=FULL) * (2.0 / width)
    freqs = jnp.power(jnp.float32(1000000.0), -steps)
    angles = places.astype(FULL)[:, None] * freqs[None, :]
    return jnp.cos(angles)[:, None, :], jnp.sin(angles)[:, None, :]


def rotate(values, cosine, sine):
    half = values.shape[-1] // 2
    first = values[..., :half]
    second = values[..., half:]
    return jnp.concatenate(
        [first * cosine - second * sine, second * cosine + first * sine], axis=-1
    )


def pick(array, index, axis):
    return lax.dynamic_index_in_dim(array, index, axis, keepdims=False)


def ordered(mine, other, bit, axis):
    first = bit == 0
    return jnp.stack([jnp.where(first, mine, other), jnp.where(first, other, mine)], axis=axis)


def after(array, *others):
    return lax.optimization_barrier((array,) + others)[0]


class Plan:
    def __init__(self, mesh):
        self.dp = mesh.shape["dp"]
        self.tensor = mesh.shape["tensor"]
        self.devices = self.dp * self.tensor
        self.lines = self.dp // 2
        self.stride = 2 * self.tensor
        self.core_mask = 1
        self.row_mask = self.tensor // 2
        self.pair_mask = self.tensor

    def here(self):
        dp = lax.axis_index("dp")
        tensor = lax.axis_index("tensor")
        self.line = dp // 2
        self.pair = dp % 2
        self.row = tensor // 2
        self.core = tensor % 2

    def swap(self, array, mask):
        return lax.ppermute(array, AXES, [(i, i ^ mask) for i in range(self.devices)])

    def groups(self):
        return [
            [line * 2 + pair for line in range(self.lines)] for pair in range(2)
        ]

    def gather_lines(self, array):
        return lax.all_gather(array, "dp", axis=0, tiled=True, axis_index_groups=self.groups())

    def sum_lines(self, parts):
        return lax.psum_scatter(
            parts, "dp", scatter_dimension=0, tiled=True, axis_index_groups=self.groups()
        )

    def gather_lines_direct(self, array):
        count = self.lines
        if count > 4:
            return lax.all_gather(array, "dp", axis=0, axis_index_groups=self.groups())
        whole = lax.dynamic_update_index_in_dim(
            jnp.zeros((count,) + array.shape, array.dtype), array, self.line, 0
        )
        others = [self.swap(array, away * self.stride) for away in range(1, count)]
        for away, other in enumerate(others, 1):
            whole = lax.dynamic_update_index_in_dim(whole, other, self.line ^ away, 0)
        return whole

    def sum_lines_direct(self, parts):
        count = self.lines
        if count > 4:
            return lax.psum_scatter(
                parts, "dp", scatter_dimension=0, axis_index_groups=self.groups()
            ).astype(FULL)
        others = [
            self.swap(pick(parts, self.line ^ away, 0), away * self.stride)
            for away in range(1, count)
        ]
        return sum([other.astype(FULL) for other in others], pick(parts, self.line, 0).astype(FULL))

    def gather_rows(self, array):
        array = ordered(array, self.swap(array, self.row_mask), self.row, 0)
        array = ordered(array, self.swap(array, self.core_mask), self.core, 1)
        return array.reshape((-1,) + array.shape[3:])

    def gather_group(self, array):
        row, pair, both = [
            self.swap(array, mask)
            for mask in (self.row_mask, self.pair_mask, self.row_mask | self.pair_mask)
        ]
        array = ordered(
            ordered(array, row, self.row, 0), ordered(pair, both, self.row, 0), self.pair, 0
        )
        array = ordered(array, self.swap(array, self.core_mask), self.core, 2)
        return array.reshape((-1,) + array.shape[4:])

    def halve(self, array, mask, bit, axis):
        other = self.swap(pick(array, 1 - bit, axis).astype(LOW), mask)
        return pick(array, bit, axis).astype(FULL) + other.astype(FULL)

    def scatter_rows(self, array):
        array = array.reshape((2, 2, -1) + array.shape[1:])
        array = self.halve(array, self.core_mask, self.core, 1)
        return self.halve(array, self.row_mask, self.row, 0)

    def scatter_group(self, array):
        array = array.reshape((2, 2, 2, -1) + array.shape[1:])
        array = self.halve(array, self.core_mask, self.core, 2).astype(LOW)

        def part(pair, row):
            return pick(pick(array, pair, 0), row, 0)

        others = [
            self.swap(part(1 - self.pair, 1 - self.row), self.pair_mask | self.row_mask),
            self.swap(part(1 - self.pair, self.row), self.pair_mask),
            self.swap(part(self.pair, 1 - self.row), self.row_mask),
        ]
        return sum([other.astype(FULL) for other in others], part(self.pair, self.row).astype(FULL))

    def sum_all(self, array):
        mask = 1
        while mask < self.devices:
            array = array + self.swap(array, mask)
            mask *= 2
        return array


def wide_of(columns):
    half = columns // 2
    return -(-half // LANES) * LANES


def channel_part(weight, owner):
    columns = weight.shape[1]
    half, wide = columns // 2, wide_of(columns)
    offset = columns - wide
    window = jnp.where(owner == 0, weight[:, :wide], weight[:, offset:])
    place = lax.broadcasted_iota(jnp.int32, window.shape, 1) + jnp.where(owner == 0, 0, offset)
    return jnp.where((place < half) == (owner == 0), window, jnp.zeros_like(window))


def spread_channels(plan, weights):
    mine, theirs = [
        jnp.concatenate([channel_part(weight, owner) for weight in weights], axis=1)
        for owner in (plan.pair, 1 - plan.pair)
    ]
    both = ordered(mine, plan.swap(theirs, plan.pair_mask), plan.pair, 0)
    return both.reshape((-1, both.shape[-1]))


def collect_channels(plan, summed, columns):
    wide = wide_of(columns)
    summed = summed.reshape((2, -1, summed.shape[1]))
    other = plan.swap(pick(summed, 1 - plan.pair, 0), plan.pair_mask).astype(FULL)
    mine = pick(summed, plan.pair, 0).astype(FULL)
    first = jnp.where(plan.pair == 0, mine, other)
    second = jnp.where(plan.pair == 0, other, mine)
    offset = columns - wide
    results = []
    for start in range(0, summed.shape[2], wide):
        low, high = first[:, start : start + wide], second[:, start : start + wide]
        results.append(
            jnp.concatenate(
                [
                    low[:, :offset],
                    low[:, offset:] + high[:, : wide - offset],
                    high[:, wide - offset :],
                ],
                axis=1,
            )
        )
    return results


def gather_model(plan, weight):
    lines = plan.gather_lines_direct(weight)
    both = ordered(lines, plan.swap(lines, plan.pair_mask), plan.pair, 1)
    return both.reshape((-1, both.shape[-1]))


def scatter_model(plan, grad):
    grad = grad.astype(LOW).reshape((plan.lines, 2, -1, grad.shape[1]))
    grad = plan.halve(grad, plan.pair_mask, plan.pair, 1).astype(LOW)
    return plan.sum_lines_direct(grad)


def body(
    plan,
    tokens,
    segment_ids,
    positions,
    norm_in_gain,
    w_query,
    w_key,
    w_value,
    query_gain,
    key_gain,
    w_output,
    norm_mid_gain,
    w_gate,
    w_up,
    w_down,
    grad_out,
):
    plan.here()
    head_dim = query_gain.shape[0]
    scaling = head_dim ** (-0.5)
    sequences, length = segment_ids.shape
    rows = sequences * length
    q_columns, k_columns = w_query.shape[1], w_key.shape[1]
    heads = q_columns // head_dim
    groups = k_columns // head_dim
    repeat = heads // groups
    channels = w_gate.shape[1]

    qkv_columns = q_columns + 2 * k_columns
    wide = wide_of(channels)

    model_full = gather_model(
        plan, jnp.concatenate([w_query, w_key, w_value, w_output.T], axis=1)
    )
    qkv_full = model_full[:, :qkv_columns]
    output_own = model_full[:, qkv_columns:]
    tokens_seq = plan.gather_rows(tokens)
    windows = spread_channels(plan, [w_gate, w_up, w_down.T])
    gate_up_full = plan.gather_lines(windows[:, : 2 * wide])
    down_full = plan.gather_lines(windows[:, 2 * wide :])
    back_group = plan.gather_group(grad_out)

    inputs = tokens_seq.astype(FULL)
    scaled_in = inputs * scale_of(inputs)
    rows_in = (scaled_in * norm_in_gain).astype(LOW)
    qkv = matmul(rows_in, qkv_full)
    query_raw = qkv[:, :q_columns]
    key_raw = qkv[:, q_columns : q_columns + k_columns]
    value_low = qkv[:, q_columns + k_columns :].astype(LOW)
    cosine, sine = angles_of(positions.reshape(rows), head_dim)

    def heads_local(query_in, key_in, query_scale, key_scale):
        query_out = rotate(
            normalize(query_in.reshape(rows, heads, head_dim), query_scale), cosine, sine
        )
        key_out = rotate(normalize(key_in.reshape(rows, groups, head_dim), key_scale), cosine, sine)
        return (query_out, key_out)

    (query_rot, key_rot), pull_heads = jax.vjp(
        heads_local, query_raw, key_raw, query_gain, key_gain
    )
    query_low = query_rot.astype(LOW).reshape(sequences, length, groups, repeat, head_dim)
    key_low = key_rot.astype(LOW).reshape(sequences, length, groups, head_dim)
    value_seq = value_low.reshape(sequences, length, groups, head_dim)

    def forward_one(query, key, value, segment):
        scores = (
            jnp.einsum("qgrd,kgd->grqk", query, key, preferred_element_type=FULL) * scaling
        )
        index = jnp.arange(length)
        allowed = (segment[:, None] == segment[None, :]) & (index[None, :] <= index[:, None])
        scores = jnp.where(allowed, scores, -1e30)
        weights = jnp.exp(scores - jnp.max(scores, axis=-1, keepdims=True))
        probs = weights / jnp.sum(weights, axis=-1, keepdims=True)
        result = jnp.einsum("grqk,kgd->qgrd", probs.astype(LOW), value, preferred_element_type=FULL)
        return (result, probs)

    attended, probs_all = jax.vmap(forward_one)(query_low, key_low, value_seq, segment_ids)
    attended_low = attended.reshape(rows, heads * head_dim).astype(LOW)
    attn_part = plan.scatter_rows(matmul_back(attended_low, output_own).astype(LOW))

    middle = tokens.astype(FULL) + attn_part
    scaled_mid = middle * scale_of(middle)
    rows_mid = plan.gather_group((scaled_mid * norm_mid_gain).astype(LOW))
    gate_up = matmul(rows_mid, gate_up_full)
    gate_value, up_value = gate_up[:, :wide], gate_up[:, wide:]
    logistic = jax.nn.sigmoid(gate_value)
    swish = gate_value * logistic
    hidden_low = (swish * up_value).astype(LOW)
    grad_down = matmul_rows(back_group, hidden_low).astype(LOW)
    down_sum = plan.sum_lines(grad_down)
    grad_hidden = matmul(back_group, after(down_full, grad_down))
    grad_gate_low = (
        grad_hidden * up_value * logistic * (1.0 + gate_value * (1.0 - logistic))
    ).astype(LOW)
    grad_up_low = (grad_hidden * swish).astype(LOW)
    grad_gate_up = jnp.concatenate([grad_gate_low, grad_up_low], axis=1)
    grad_normed_mid = plan.scatter_group(matmul_back(grad_gate_up, gate_up_full).astype(LOW))
    gain_mid = jnp.sum(grad_normed_mid * scaled_mid, axis=0)
    upstream = grad_out.astype(FULL)
    grad_middle = upstream + normalize_back(middle, norm_mid_gain, grad_normed_mid)
    rows_attn_back = plan.gather_rows(grad_middle.astype(LOW))

    gate_up_sum = plan.sum_lines(matmul_rows(rows_mid, grad_gate_up).astype(LOW))
    mlp_part = plan.scatter_group(matmul_back(hidden_low, down_full).astype(LOW))
    block_out = (middle + mlp_part).astype(LOW)
    (summed_down,) = collect_channels(plan, down_sum, channels)
    summed_gate, summed_up = collect_channels(plan, gate_up_sum, channels)

    grad_attended = matmul(rows_attn_back, output_own).astype(LOW)
    summed_output = scatter_model(plan, matmul_rows(rows_attn_back, attended_low)).T

    def backward_one(query, key, value, probs, grad_result):
        grad_probs = jnp.einsum("qgrd,kgd->grqk", grad_result, value, preferred_element_type=FULL)
        inner = jnp.sum(probs * grad_probs, axis=-1, keepdims=True)
        grad_scores = (probs * (grad_probs - inner)).astype(LOW)
        grad_query = (
            jnp.einsum("grqk,kgd->qgrd", grad_scores, key, preferred_element_type=FULL) * scaling
        )
        grad_key = (
            jnp.einsum("grqk,qgrd->kgd", grad_scores, query, preferred_element_type=FULL) * scaling
        )
        grad_value = jnp.einsum(
            "grqk,qgrd->kgd", probs.astype(LOW), grad_result, preferred_element_type=FULL
        )
        return (grad_query, grad_key, grad_value)

    grad_heads = grad_attended.reshape(sequences, length, groups, repeat, head_dim)
    grad_query_all, grad_key_all, grad_value_all = jax.vmap(backward_one)(
        query_low, key_low, value_seq, probs_all, grad_heads
    )
    grad_query_raw, grad_key_raw, grad_query_scale, grad_key_scale = pull_heads(
        (
            grad_query_all.reshape(rows, heads, head_dim),
            grad_key_all.reshape(rows, groups, head_dim),
        )
    )
    grad_qkv = jnp.concatenate(
        [
            grad_query_raw.astype(LOW),
            grad_key_raw.astype(LOW),
            grad_value_all.reshape(rows, k_columns).astype(LOW),
        ],
        axis=1,
    )
    summed_model = scatter_model(plan, matmul_rows(rows_in, grad_qkv))
    in_part = matmul_back(grad_qkv, qkv_full)
    gain_in = jnp.sum(in_part * scaled_in, axis=0)
    grad_normed_in = plan.scatter_rows(in_part.astype(LOW))
    grad_tokens = (
        grad_middle + normalize_back(tokens.astype(FULL), norm_in_gain, grad_normed_in)
    ).astype(LOW)

    gains = plan.sum_all(
        jnp.concatenate([gain_in, gain_mid, grad_query_scale, grad_key_scale])
    )
    width = gain_in.shape[0]
    return (
        block_out,
        grad_tokens,
        gains[:width],
        summed_model[:, :q_columns],
        summed_model[:, q_columns : q_columns + k_columns],
        summed_model[:, q_columns + k_columns :],
        gains[2 * width : 2 * width + head_dim],
        gains[2 * width + head_dim :],
        summed_output,
        gains[width : 2 * width],
        summed_gate,
        summed_up,
        summed_down.T,
    )


def solution(mesh):
    plan = Plan(mesh)

    def step(*args):
        return body(plan, *args)

    return jax.shard_map(
        step,
        mesh=mesh,
        in_specs=(
            P(("dp", "tensor"), None),
            P("dp", None),
            P("dp", None),
            P(),
            P("dp", "tensor"),
            P("dp", "tensor"),
            P("dp", "tensor"),
            P(),
            P(),
            P("tensor", "dp"),
            P(),
            P("dp", "tensor"),
            P("dp", "tensor"),
            P("tensor", "dp"),
            P(("dp", "tensor"), None),
        ),
        out_specs=(
            P(("dp", "tensor"), None),
            P(("dp", "tensor"), None),
            P(),
            P("dp", "tensor"),
            P("dp", "tensor"),
            P("dp", "tensor"),
            P(),
            P(),
            P("tensor", "dp"),
            P(),
            P("dp", "tensor"),
            P("dp", "tensor"),
            P("tensor", "dp"),
        ),
        check_vma=False,
    )
```

```python
import jax
import jax.numpy as jnp
from jax import lax
from jax.sharding import PartitionSpec as P

EPSILON = 1e-05
AXES = ("dp", "tensor")
LOW = jnp.bfloat16
FULL = jnp.float32
LANES = 128


def matmul(left, right):
    return jnp.dot(left, right, preferred_element_type=FULL)


def matmul_back(left, right):
    return lax.dot_general(left, right, (((1,), (1,)), ((), ())), preferred_element_type=FULL)


def matmul_rows(left, right):
    return lax.dot_general(left, right, (((0,), (0,)), ((), ())), preferred_element_type=FULL)


def scale_of(values):
    return lax.rsqrt(jnp.mean(values * values, axis=-1, keepdims=True) + EPSILON)


def normalize(values, gain):
    return values * scale_of(values) * gain


def normalize_back(values, gain, grad):
    scale = scale_of(values)
    grad = grad * gain
    inner = jnp.mean(grad * values, axis=-1, keepdims=True)
    return scale * grad - values * (scale * scale * scale * inner)


def angles_of(places, width):
    half = width // 2
    steps = jnp.arange(half, dtype=FULL) * (2.0 / width)
    freqs = jnp.power(jnp.float32(1000000.0), -steps)
    angles = places.astype(FULL)[:, None] * freqs[None, :]
    return jnp.cos(angles)[:, None, :], jnp.sin(angles)[:, None, :]


def rotate(values, cosine, sine):
    half = values.shape[-1] // 2
    first = values[..., :half]
    second = values[..., half:]
    return jnp.concatenate(
        [first * cosine - second * sine, second * cosine + first * sine], axis=-1
    )


def pick(array, index, axis):
    return lax.dynamic_index_in_dim(array, index, axis, keepdims=False)


def ordered(mine, other, bit, axis):
    first = bit == 0
    return jnp.stack([jnp.where(first, mine, other), jnp.where(first, other, mine)], axis=axis)


def after(array, *others):
    return lax.optimization_barrier((array,) + others)[0]


class Plan:
    def __init__(self, mesh):
        self.dp = mesh.shape["dp"]
        self.tensor = mesh.shape["tensor"]
        self.devices = self.dp * self.tensor
        self.lines = self.dp // 2
        self.stride = 2 * self.tensor
        self.core_mask = 1
        self.row_mask = self.tensor // 2
        self.pair_mask = self.tensor

    def here(self):
        dp = lax.axis_index("dp")
        tensor = lax.axis_index("tensor")
        self.line = dp // 2
        self.pair = dp % 2
        self.row = tensor // 2
        self.core = tensor % 2

    def swap(self, array, mask):
        return lax.ppermute(array, AXES, [(i, i ^ mask) for i in range(self.devices)])

    def groups(self):
        return [
            [line * 2 + pair for line in range(self.lines)] for pair in range(2)
        ]

    def gather_lines(self, array):
        return lax.all_gather(array, "dp", axis=0, tiled=True, axis_index_groups=self.groups())

    def sum_lines(self, parts):
        return lax.psum_scatter(
            parts, "dp", scatter_dimension=0, tiled=True, axis_index_groups=self.groups()
        )

    def gather_lines_direct(self, array):
        count = self.lines
        if count > 4:
            return lax.all_gather(array, "dp", axis=0, axis_index_groups=self.groups())
        whole = lax.dynamic_update_index_in_dim(
            jnp.zeros((count,) + array.shape, array.dtype), array, self.line, 0
        )
        others = [self.swap(array, away * self.stride) for away in range(1, count)]
        for away, other in enumerate(others, 1):
            whole = lax.dynamic_update_index_in_dim(whole, other, self.line ^ away, 0)
        return whole

    def sum_lines_direct(self, parts):
        count = self.lines
        if count > 4:
            return lax.psum_scatter(
                parts, "dp", scatter_dimension=0, axis_index_groups=self.groups()
            ).astype(FULL)
        others = [
            self.swap(pick(parts, self.line ^ away, 0), away * self.stride)
            for away in range(1, count)
        ]
        return sum([other.astype(FULL) for other in others], pick(parts, self.line, 0).astype(FULL))

    def gather_rows(self, array):
        array = ordered(array, self.swap(array, self.row_mask), self.row, 0)
        array = ordered(array, self.swap(array, self.core_mask), self.core, 1)
        return array.reshape((-1,) + array.shape[3:])

    def gather_group(self, array):
        row, pair, both = [
            self.swap(array, mask)
            for mask in (self.row_mask, self.pair_mask, self.row_mask | self.pair_mask)
        ]
        array = ordered(
            ordered(array, row, self.row, 0), ordered(pair, both, self.row, 0), self.pair, 0
        )
        array = ordered(array, self.swap(array, self.core_mask), self.core, 0)
        return array.reshape((-1,) + array.shape[4:])

    def halve(self, array, mask, bit, axis):
        other = self.swap(pick(array, 1 - bit, axis).astype(LOW), mask)
        return pick(array, bit, axis).astype(FULL) + other.astype(FULL)

    def scatter_rows(self, array):
        array = array.reshape((2, 2, -1) + array.shape[1:])
        array = self.halve(array, self.core_mask, self.core, 1)
        return self.halve(array, self.row_mask, self.row, 0)

    def scatter_group(self, array):
        array = array.reshape((2, 2, 2, -1) + array.shape[1:])
        array = self.halve(array, self.core_mask, self.core, 0).astype(LOW)

        def part(pair, row):
            return pick(pick(array, pair, 0), row, 0)

        others = [
            self.swap(part(1 - self.pair, 1 - self.row), self.pair_mask | self.row_mask),
            self.swap(part(1 - self.pair, self.row), self.pair_mask),
            self.swap(part(self.pair, 1 - self.row), self.row_mask),
        ]
        return sum([other.astype(FULL) for other in others], part(self.pair, self.row).astype(FULL))

    def sum_all(self, array):
        mask = 1
        while mask < self.devices:
            array = array + self.swap(array, mask)
            mask *= 2
        return array


def wide_of(columns):
    half = columns // 2
    return -(-half // LANES) * LANES


def channel_part(weight, owner):
    columns = weight.shape[1]
    half, wide = columns // 2, wide_of(columns)
    offset = columns - wide
    window = jnp.where(owner == 0, weight[:, :wide], weight[:, offset:])
    place = lax.broadcasted_iota(jnp.int32, window.shape, 1) + jnp.where(owner == 0, 0, offset)
    return jnp.where((place < half) == (owner == 0), window, jnp.zeros_like(window))


def spread_channels(plan, weights):
    mine, theirs = [
        jnp.concatenate([channel_part(weight, owner) for weight in weights], axis=1)
        for owner in (plan.pair, 1 - plan.pair)
    ]
    both = ordered(mine, plan.swap(theirs, plan.pair_mask), plan.pair, 0)
    return both.reshape((-1, both.shape[-1]))


def collect_channels(plan, summed, columns):
    wide = wide_of(columns)
    summed = summed.reshape((2, -1, summed.shape[1]))
    other = plan.swap(pick(summed, 1 - plan.pair, 0), plan.pair_mask).astype(FULL)
    mine = pick(summed, plan.pair, 0).astype(FULL)
    first = jnp.where(plan.pair == 0, mine, other)
    second = jnp.where(plan.pair == 0, other, mine)
    offset = columns - wide
    results = []
    for start in range(0, summed.shape[2], wide):
        low, high = first[:, start : start + wide], second[:, start : start + wide]
        results.append(
            jnp.concatenate(
                [
                    low[:, :offset],
                    low[:, offset:] + high[:, : wide - offset],
                    high[:, wide - offset :],
                ],
                axis=1,
            )
        )
    return results


def gather_model(plan, weight):
    lines = plan.gather_lines_direct(weight)
    both = ordered(lines, plan.swap(lines, plan.pair_mask), plan.pair, 1)
    return both.reshape((-1, both.shape[-1]))


def scatter_model(plan, grad):
    grad = grad.astype(LOW).reshape((plan.lines, 2, -1, grad.shape[1]))
    grad = plan.halve(grad, plan.pair_mask, plan.pair, 1).astype(LOW)
    return plan.sum_lines_direct(grad)


def body(
    plan,
    tokens,
    segment_ids,
    positions,
    norm_in_gain,
    w_query,
    w_key,
    w_value,
    query_gain,
    key_gain,
    w_output,
    norm_mid_gain,
    w_gate,
    w_up,
    w_down,
    grad_out,
):
    plan.here()
    head_dim = query_gain.shape[0]
    scaling = head_dim ** (-0.5)
    sequences, length = segment_ids.shape
    rows = sequences * length
    q_columns, k_columns = w_query.shape[1], w_key.shape[1]
    heads = q_columns // head_dim
    groups = k_columns // head_dim
    repeat = heads // groups
    channels = w_gate.shape[1]

    qkv_columns = q_columns + 2 * k_columns
    wide = wide_of(channels)

    model_full = gather_model(
        plan, jnp.concatenate([w_query, w_key, w_value, w_output.T], axis=1)
    )
    qkv_full = model_full[:, :qkv_columns]
    output_own = model_full[:, qkv_columns:]
    tokens_seq = plan.gather_rows(tokens)
    windows = spread_channels(plan, [w_gate, w_up, w_down.T])
    gate_up_full = plan.gather_lines(windows[:, : 2 * wide])
    down_full = plan.gather_lines(windows[:, 2 * wide :])
    back_group = plan.gather_group(grad_out)

    inputs = tokens_seq.astype(FULL)
    scaled_in = inputs * scale_of(inputs)
    rows_in = (scaled_in * norm_in_gain).astype(LOW)
    qkv = matmul(rows_in, qkv_full)
    query_raw = qkv[:, :q_columns]
    key_raw = qkv[:, q_columns : q_columns + k_columns]
    value_low = qkv[:, q_columns + k_columns :].astype(LOW)
    cosine, sine = angles_of(positions.reshape(rows), head_dim)

    def heads_local(query_in, key_in, query_scale, key_scale):
        query_out = rotate(
            normalize(query_in.reshape(rows, heads, head_dim), query_scale), cosine, sine
        )
        key_out = rotate(normalize(key_in.reshape(rows, groups, head_dim), key_scale), cosine, sine)
        return (query_out, key_out)

    (query_rot, key_rot), pull_heads = jax.vjp(
        heads_local, query_raw, key_raw, query_gain, key_gain
    )
    query_low = query_rot.astype(LOW).reshape(sequences, length, groups, repeat, head_dim)
    key_low = key_rot.astype(LOW).reshape(sequences, length, groups, head_dim)
    value_seq = value_low.reshape(sequences, length, groups, head_dim)

    def forward_one(query, key, value, segment):
        scores = (
            jnp.einsum("qgrd,kgd->grqk", query, key, preferred_element_type=FULL) * scaling
        )
        index = jnp.arange(length)
        allowed = (segment[:, None] == segment[None, :]) & (index[None, :] <= index[:, None])
        scores = jnp.where(allowed, scores, -1e30)
        weights = jnp.exp(scores - jnp.max(scores, axis=-1, keepdims=True))
        probs = weights / jnp.sum(weights, axis=-1, keepdims=True)
        result = jnp.einsum("grqk,kgd->qgrd", probs.astype(LOW), value, preferred_element_type=FULL)
        return (result, probs)

    attended, probs_all = jax.vmap(forward_one)(query_low, key_low, value_seq, segment_ids)
    attended_low = attended.reshape(rows, heads * head_dim).astype(LOW)
    attn_part = plan.scatter_rows(matmul_back(attended_low, output_own).astype(LOW))

    middle = tokens.astype(FULL) + attn_part
    scaled_mid = middle * scale_of(middle)
    rows_mid = plan.gather_group((scaled_mid * norm_mid_gain).astype(LOW))
    gate_up = matmul(rows_mid, gate_up_full)
    gate_value, up_value = gate_up[:, :wide], gate_up[:, wide:]
    logistic = jax.nn.sigmoid(gate_value)
    swish = gate_value * logistic
    hidden_low = (swish * up_value).astype(LOW)
    grad_down = matmul_rows(back_group, hidden_low).astype(LOW)
    down_sum = plan.sum_lines(grad_down)
    grad_hidden = matmul(back_group, after(down_full, grad_down))
    grad_gate_low = (
        grad_hidden * up_value * logistic * (1.0 + gate_value * (1.0 - logistic))
    ).astype(LOW)
    grad_up_low = (grad_hidden * swish).astype(LOW)
    grad_gate_up = jnp.concatenate([grad_gate_low, grad_up_low], axis=1)
    grad_normed_mid = plan.scatter_group(matmul_back(grad_gate_up, gate_up_full).astype(LOW))
    gain_mid = jnp.sum(grad_normed_mid * scaled_mid, axis=0)
    upstream = grad_out.astype(FULL)
    grad_middle = upstream + normalize_back(middle, norm_mid_gain, grad_normed_mid)
    rows_attn_back = plan.gather_rows(grad_middle.astype(LOW))

    gate_up_sum = plan.sum_lines(matmul_rows(rows_mid, grad_gate_up).astype(LOW))
    mlp_part = plan.scatter_group(matmul_back(hidden_low, down_full).astype(LOW))
    block_out = (middle + mlp_part).astype(LOW)
    (summed_down,) = collect_channels(plan, down_sum, channels)
    summed_gate, summed_up = collect_channels(plan, gate_up_sum, channels)

    grad_attended = matmul(rows_attn_back, output_own).astype(LOW)
    summed_output = scatter_model(plan, matmul_rows(rows_attn_back, attended_low)).T

    def backward_one(query, key, value, probs, grad_result):
        grad_probs = jnp.einsum("qgrd,kgd->grqk", grad_result, value, preferred_element_type=FULL)
        inner = jnp.sum(probs * grad_probs, axis=-1, keepdims=True)
        grad_scores = (probs * (grad_probs - inner)).astype(LOW)
        grad_query = (
            jnp.einsum("grqk,kgd->qgrd", grad_scores, key, preferred_element_type=FULL) * scaling
        )
        grad_key = (
            jnp.einsum("grqk,qgrd->kgd", grad_scores, query, preferred_element_type=FULL) * scaling
        )
        grad_value = jnp.einsum(
            "grqk,qgrd->kgd", probs.astype(LOW), grad_result, preferred_element_type=FULL
        )
        return (grad_query, grad_key, grad_value)

    grad_heads = grad_attended.reshape(sequences, length, groups, repeat, head_dim)
    grad_query_all, grad_key_all, grad_value_all = jax.vmap(backward_one)(
        query_low, key_low, value_seq, probs_all, grad_heads
    )
    grad_query_raw, grad_key_raw, grad_query_scale, grad_key_scale = pull_heads(
        (
            grad_query_all.reshape(rows, heads, head_dim),
            grad_key_all.reshape(rows, groups, head_dim),
        )
    )
    grad_qkv = jnp.concatenate(
        [
            grad_query_raw.astype(LOW),
            grad_key_raw.astype(LOW),
            grad_value_all.reshape(rows, k_columns).astype(LOW),
        ],
        axis=1,
    )
    summed_model = scatter_model(plan, matmul_rows(rows_in, grad_qkv))
    in_part = matmul_back(grad_qkv, qkv_full)
    gain_in = jnp.sum(in_part * scaled_in, axis=0)
    grad_normed_in = plan.scatter_rows(in_part.astype(LOW))
    grad_tokens = (
        grad_middle + normalize_back(tokens.astype(FULL), norm_in_gain, grad_normed_in)
    ).astype(LOW)

    gains = plan.sum_all(
        jnp.concatenate([gain_in, gain_mid, grad_query_scale, grad_key_scale])
    )
    width = gain_in.shape[0]
    return (
        block_out,
        grad_tokens,
        gains[:width],
        summed_model[:, :q_columns],
        summed_model[:, q_columns : q_columns + k_columns],
        summed_model[:, q_columns + k_columns :],
        gains[2 * width : 2 * width + head_dim],
        gains[2 * width + head_dim :],
        summed_output,
        gains[width : 2 * width],
        summed_gate,
        summed_up,
        summed_down.T,
    )


def solution(mesh):
    plan = Plan(mesh)

    def step(*args):
        return body(plan, *args)

    return jax.shard_map(
        step,
        mesh=mesh,
        in_specs=(
            P(("dp", "tensor"), None),
            P("dp", None),
            P("dp", None),
            P(),
            P("dp", "tensor"),
            P("dp", "tensor"),
            P("dp", "tensor"),
            P(),
            P(),
            P("tensor", "dp"),
            P(),
            P("dp", "tensor"),
            P("dp", "tensor"),
            P("tensor", "dp"),
            P(("dp", "tensor"), None),
        ),
        out_specs=(
            P(("dp", "tensor"), None),
            P(("dp", "tensor"), None),
            P(),
            P("dp", "tensor"),
            P("dp", "tensor"),
            P("dp", "tensor"),
            P(),
            P(),
            P("tensor", "dp"),
            P(),
            P("dp", "tensor"),
            P("dp", "tensor"),
            P("tensor", "dp"),
        ),
        check_vma=False,
    )
```
